512 devices in a mesh: dp: 16 (over x_lo, y, core), tensor: 32 (over z, x_hi).
Axes of the slice: x: 4 (x_hi: 2, x_lo: 2; x = x_hi * 2 + x_lo), y: 4, z: 16, core: 2. Of those that a mesh axis runs over, the one named last changes fastest.
Arguments:
- tokens: bfloat16 [2048, 8192], P(('dp', 'tensor')), may hold values from -6 to 6
- gate_weight: bfloat16 [8192, 28672], P('dp', 'tensor'), may hold values from -0.0625 to 0.0625
- up_weight: bfloat16 [8192, 28672], P('dp', 'tensor'), may hold values from -0.0625 to 0.0625
- hidden_grad: bfloat16 [2048, 28672], P('dp', 'tensor'), may hold values from -1.5 to 1.5
Outputs:
- hidden: bfloat16 [2048, 28672], P('dp', 'tensor')
- tokens_grad: bfloat16 [2048, 8192], P(('dp', 'tensor'))
- gate_grad: bfloat16 [8192, 28672], P('dp', 'tensor')
- up_grad: bfloat16 [8192, 28672], P('dp', 'tensor')
The draws below stay inside these ranges and needn't reach their ends.
All inputs are finite; a program needn't handle non-finite values.
Results may differ from the reference program's by a relative error of at most 0.0049.
Values may be sent and summed in bfloat16 or wider, within the bound.
A program may use at most 128 MiB of HBM per device.

```python
import jax
import jax.numpy as jnp

D = 8192
FF = 28672
TOKENS = 2048


def shard_levels(own_key, shape, split, smallest, top_value):
    factor_of = 1.0
    for position, parts in split:
        heights = jax.random.uniform(jax.random.fold_in(jax.random.fold_in(own_key, 6), position), (parts,), jnp.float32, smallest / len(split), top_value / len(split))
        factor_of = factor_of * jnp.repeat(jnp.exp(heights), shape[position] // parts).reshape((-1,) + (1,) * (len(shape) - 1 - position))
    return factor_of


def scatter_about(own_key, dims, width, most, pieces=(), dtype=jnp.bfloat16):
    gain = shard_levels(own_key, dims, pieces, -0.22, 0.18) if pieces else 1.0
    array = jax.random.normal(own_key, dims, jnp.float32) * width * gain
    return jnp.minimum(jnp.maximum(array, -most), most).astype(dtype)


def setup_inputs(seed: int = 0) -> dict:
    splits = jax.random.split(jax.random.key(seed), 5)
    tokens = scatter_about(splits[0], (TOKENS, D), 1.0, 6.0, ((0, 512),))
    gate_weight = scatter_about(splits[1], (D, FF), D ** -0.5, 0.0625, ((0, 16), (1, 32)))
    up_weight = scatter_about(splits[2], (D, FF), D ** -0.5, 0.0625, ((0, 16), (1, 32)))
    hidden_grad = scatter_about(splits[3], (TOKENS, FF), 0.25, 1.5, ((0, 16), (1, 32)))
    return dict(tokens=tokens, gate_weight=gate_weight, up_weight=up_weight, hidden_grad=hidden_grad)


def reference(tokens, gate_weight, up_weight, hidden_grad):
    gate = jnp.dot(tokens, gate_weight, preferred_element_type=jnp.float32)
    up = jnp.dot(tokens, up_weight, preferred_element_type=jnp.float32)
    sig = jax.nn.sigmoid(gate)
    act = gate * sig
    hidden = (act * up).astype(jnp.bfloat16)
    cot = hidden_grad.astype(jnp.float32)
    gate_delta = (cot * up * sig * (1.0 + gate * (1.0 - sig))).astype(jnp.bfloat16)
    up_delta = (cot * act).astype(jnp.bfloat16)
    tokens_grad = jnp.dot(gate_delta, gate_weight.T, preferred_element_type=jnp.float32)
    tokens_grad = tokens_grad + jnp.dot(up_delta, up_weight.T, preferred_element_type=jnp.float32)
    gate_sum = jnp.dot(tokens.T, gate_delta, preferred_element_type=jnp.float32)
    up_sum = jnp.dot(tokens.T, up_delta, preferred_element_type=jnp.float32)
    return hidden, tokens_grad.astype(jnp.bfloat16), gate_sum.astype(jnp.bfloat16), up_sum.astype(jnp.bfloat16)
```

```python
import functools

import jax
import jax.numpy as jnp
from jax import lax
from jax.experimental import pallas as pl
from jax.experimental.pallas import tpu as pltpu
from jax.sharding import PartitionSpec as P

MESH = pl.DeviceIdType.MESH
F32 = jnp.float32
BF16 = jnp.bfloat16
NZ = 16
NS = 8
CUT = 512
FIRST = 1
LOW = 3


def send(src, dst, send_sem, recv_sem, device):
    pltpu.make_async_remote_copy(
        src_ref=src,
        dst_ref=dst,
        send_sem=send_sem,
        recv_sem=recv_sem,
        device_id=device,
        device_id_type=MESH,
    ).start()


def take(ref, sem):
    pltpu.make_async_copy(ref, ref, sem).wait()


def kernel(
    tok_ref, gw_ref, uw_ref, hg_ref,
    hid_ref, tg_ref, gg_ref, ug_ref,
    wbuf, ts, ta, tb, asm, xbuf, xpt,
    sbuf, fbuf, gya, ux, gyb, gxs, gxr, gown, uacc, us, uya0, uya1, uyb,
    dbuf, pbuf, zacc, zs, zr, zsl, zrl,
    fs, fr, fown, ps, pr, ws, wr, wown,
    w_local, w_send, w_recv, t_send, t_recv, h_send, h_recv, az_send, az_recv,
    ssem, rsem, z_send, z_recv, zl_send, zl_recv, f_send, f_recv, p_send, p_recv, ww_send, ww_recv,
):
    dp, tensor = lax.axis_index("dp"), lax.axis_index("tensor")
    core = lax.rem(dp, 2)
    p = dp // 2
    y, xl = lax.rem(p, 4), p // 4
    xh, z = lax.rem(tensor, 2), tensor // 2
    yp, y2, ym = lax.rem(y + 1, 4), lax.rem(y + 2, 4), lax.rem(y + 3, 4)
    xo = 1 - xl

    def at(xx, yy):
        return ((xx * 4 + yy) * 2 + core, tensor)

    up_y, down_y, over_x = at(xl, yp), at(xl, ym), at(xo, y)
    up_z = (dp, lax.rem(z + 1, NZ) * 2 + xh)
    down_z = (dp, lax.rem(z + NZ - 1, NZ) * 2 + xh)
    over_h = (dp, z * 2 + (1 - xh))
    over_c = (p * 2 + (1 - core), tensor)

    half = gw_ref.shape[0]
    cols = gw_ref.shape[1]
    dc = 2 * half
    gate_c, up_c = pl.ds(0, cols), pl.ds(cols, cols)
    n_w = 2 * cols // 256

    barrier = pltpu.get_barrier_semaphore()
    for j in range(1, 8):
        g = lax.rem(p + j, 8)
        pl.semaphore_signal(barrier, inc=1, device_id=(g * 2 + core, tensor), device_id_type=MESH)
    for other in (up_z, down_z, over_h, over_c):
        pl.semaphore_signal(barrier, inc=1, device_id=other, device_id_type=MESH)
    for g in range(8):
        ts[g] = tok_ref[:, g * dc : (g + 1) * dc]
    pl.semaphore_wait(barrier, 11)

    for j in range(1, 8):
        g = lax.rem(p + j, 8)
        send(ts.at[g], ta.at[p], t_send.at[j], t_recv.at[j], (g * 2 + core, tensor))
    mine = pl.ds(pl.multiple_of(core * half, half), half)
    for m, (w_ref, c) in enumerate(((gw_ref, gate_c), (uw_ref, up_c))):
        pltpu.make_async_copy(w_ref, wbuf.at[mine, c], w_local.at[m]).start()
        send(w_ref, wbuf.at[mine, c], w_send.at[m], w_recv.at[m], over_c)
    ta[p] = ts[p]
    for j in range(1, 8):
        take(ta.at[lax.rem(p + 8 - j, 8)], t_recv.at[j])
    send(ta, tb, h_send, h_recv, over_h)
    take(tb, h_recv)
    for g in range(8):
        own, oth = ta[g].astype(F32), tb[g].astype(F32)
        asm[g * 8 : g * 8 + 4] = jnp.where(xh == 0, own, oth)
        asm[g * 8 + 4 : g * 8 + 8] = jnp.where(xh == 0, oth, own)
    xbuf[z] = asm[...].astype(BF16)
    send(xbuf.at[z], xbuf.at[z], az_send.at[0, 0], az_recv.at[0, 0], up_z)
    send(xbuf.at[z], xbuf.at[z], az_send.at[1, 0], az_recv.at[1, 0], down_z)

    theirs = pl.ds(pl.multiple_of((1 - core) * half, half), half)
    for m, c in enumerate((gate_c, up_c)):
        take(wbuf.at[mine, c], w_local.at[m])
        take(wbuf.at[theirs, c], w_recv.at[m])

    def pair_of(s):
        hop = (s + 1) // 2
        sign = 1 - 2 * lax.rem(s + z, 2)
        return lax.rem(z // 2 + sign * hop + NS, NS)

    def gather_z(s):
        lo = lax.rem(z + NZ - 1 - s, NZ)
        hi = lax.rem(z + 1 + s, NZ)
        take(xbuf.at[lo], az_recv.at[0, s])

        @pl.when(s < 7)
        def _():
            send(xbuf.at[lo], xbuf.at[lo], az_send.at[0, s + 1], az_recv.at[0, s + 1], up_z)
            take(xbuf.at[hi], az_recv.at[1, s])

        @pl.when(s < 6)
        def _():
            send(xbuf.at[hi], xbuf.at[hi], az_send.at[1, s + 1], az_recv.at[1, s + 1], down_z)

    def forward(s):
        pair = pair_of(s)
        slot = lax.rem(s, 4)
        x0 = xbuf[2 * pair].astype(F32)
        x1 = xbuf[2 * pair + 1].astype(F32)
        rows = []
        for g in range(8):
            rows += [x0[g * 8 : g * 8 + 8], x1[g * 8 : g * 8 + 8]]
        xf = jnp.concatenate(rows, axis=0)
        xp = xf.astype(BF16)
        for n in range(n_w):
            c = slice(n * 256, (n + 1) * 256)
            part = jnp.dot(xp, wbuf[:, c], preferred_element_type=F32).reshape(2, 4, 16, 256)
            fbuf[slot, :, :, :, c] = part
            sbuf[s, :, :, :, c] = part.astype(BF16)
        send(sbuf.at[s, 0, y2, :, gate_c], gya.at[s, 0], ssem.at[0, s], rsem.at[0, s], up_y)
        send(sbuf.at[s, 1, y2, :, gate_c], gya.at[s, 1], ssem.at[1, s], rsem.at[1, s], down_y)
        send(sbuf.at[s, xo, :, :, up_c], ux.at[s], ssem.at[2, s], rsem.at[2, s], over_x)
        xpt[:, pl.ds(pl.multiple_of(s * 128, 128), 128)] = xf.T.astype(BF16)

    def reduce_b(s):
        slot = lax.rem(s, 4)
        take(gya.at[s, 0], rsem.at[0, s])
        sbuf[s, 0, yp, :, :cols] = (fbuf[slot, 0, yp, :, :cols] + gya[s, 0].astype(F32)).astype(BF16)
        send(sbuf.at[s, :, yp, :, gate_c], gyb.at[s, 0], ssem.at[3, s], rsem.at[3, s], up_y)
        take(gya.at[s, 1], rsem.at[1, s])
        sbuf[s, 1, ym, :, :cols] = (fbuf[slot, 1, ym, :, :cols] + gya[s, 1].astype(F32)).astype(BF16)
        send(sbuf.at[s, :, ym, :, gate_c], gyb.at[s, 1], ssem.at[4, s], rsem.at[4, s], down_y)
        take(ux.at[s], rsem.at[2, s])
        uacc[slot] = fbuf[slot, xl, :, :, cols:] + ux[s].astype(F32)
        us[s, y2] = uacc[slot, y2].astype(BF16)
        send(us.at[s, y2, :, pl.ds(0, CUT)], uya0.at[s], ssem.at[5, s], rsem.at[5, s], up_y)
        send(us.at[s, y2, :, pl.ds(CUT, cols - CUT)], uya1.at[s], ssem.at[6, s], rsem.at[6, s], down_y)

    def reduce_c(s):
        slot = lax.rem(s, 4)
        take(gyb.at[s, 0], rsem.at[3, s])
        take(gyb.at[s, 1], rsem.at[4, s])
        gxs[s] = (
            fbuf[slot, xo, y, :, :cols] + gyb[s, 0, xo].astype(F32) + gyb[s, 1, xo].astype(F32)
        ).astype(BF16)
        send(gxs.at[s], gxr.at[s], ssem.at[7, s], rsem.at[7, s], over_x)
        gown[slot] = fbuf[slot, xl, y, :, :cols] + gyb[s, 0, xl].astype(F32) + gyb[s, 1, xl].astype(F32)
        take(uya0.at[s], rsem.at[5, s])
        us[s, yp, :, :CUT] = (uacc[slot, yp, :, :CUT] + uya0[s].astype(F32)).astype(BF16)
        us[s, yp, :, CUT:] = uacc[slot, yp, :, CUT:].astype(BF16)
        send(us.at[s, yp], uyb.at[s, 0], ssem.at[8, s], rsem.at[8, s], up_y)
        take(uya1.at[s], rsem.at[6, s])
        us[s, ym, :, CUT:] = (uacc[slot, ym, :, CUT:] + uya1[s].astype(F32)).astype(BF16)
        us[s, ym, :, :CUT] = uacc[slot, ym, :, :CUT].astype(BF16)
        send(us.at[s, ym], uyb.at[s, 1], ssem.at[9, s], rsem.at[9, s], down_y)

    def reduce_d(s):
        slot = lax.rem(s, 4)
        rows = pl.ds(pl.multiple_of(pair_of(s) * 16, 16), 16)
        take(gxr.at[s], rsem.at[7, s])
        take(uyb.at[s, 0], rsem.at[8, s])
        take(uyb.at[s, 1], rsem.at[9, s])
        gate = gown[slot] + gxr[s].astype(F32)
        up = uacc[slot, y] + uyb[s, 0].astype(F32) + uyb[s, 1].astype(F32)
        sig = jax.nn.sigmoid(gate)
        act = gate * sig
        hid_ref[rows, :] = (act * up).astype(BF16)
        cot = hg_ref[rows, :].astype(F32)
        dbuf[s, xl, y, :, :cols] = (cot * up * sig * (1.0 + gate * (1.0 - sig))).astype(BF16)
        dbuf[s, xl, y, :, cols:] = (cot * act).astype(BF16)

    def order(i):
        return jnp.where(i < FIRST, i, NS - 1 + FIRST - i)

    def same(ref, kind, s, device):
        send(ref, ref, ssem.at[kind, s], rsem.at[kind, s], device)

    c_lo, c_hi = pl.ds(cols, CUT), pl.ds(cols + CUT, cols - CUT)

    def spread_a(s):
        same(dbuf.at[s, xl, y, :, up_c], 11, s, up_y)
        same(dbuf.at[s, xl, y, :, up_c], 12, s, down_y)
        same(dbuf.at[s, xl, y, :, gate_c], 10, s, over_x)

    def spread_b(s):
        take(dbuf.at[s, xo, y, :, gate_c], rsem.at[10, s])
        same(dbuf.at[s, :, y, :, gate_c], 13, s, up_y)
        same(dbuf.at[s, :, y, :, gate_c], 14, s, down_y)
        take(dbuf.at[s, xl, ym, :, up_c], rsem.at[11, s])
        same(dbuf.at[s, xl, ym, :, c_lo], 15, s, up_y)
        take(dbuf.at[s, xl, yp, :, up_c], rsem.at[12, s])
        same(dbuf.at[s, xl, yp, :, c_hi], 16, s, down_y)

    def spread_c(s):
        take(dbuf.at[s, xl, y2, :, c_lo], rsem.at[15, s])
        take(dbuf.at[s, xl, y2, :, c_hi], rsem.at[16, s])
        same(dbuf.at[s, xl, :, :, up_c], 19, s, over_x)
        take(dbuf.at[s, :, ym, :, gate_c], rsem.at[13, s])
        same(dbuf.at[s, 0, ym, :, gate_c], 17, s, up_y)
        take(dbuf.at[s, :, yp, :, gate_c], rsem.at[14, s])
        same(dbuf.at[s, 1, yp, :, gate_c], 18, s, down_y)

    def spread_d(s):
        take(dbuf.at[s, 0, y2, :, gate_c], rsem.at[17, s])
        take(dbuf.at[s, 1, y2, :, gate_c], rsem.at[18, s])
        take(dbuf.at[s, xo, :, :, up_c], rsem.at[19, s])
        pair = pair_of(s)
        delta = dbuf[s].reshape(128, 2 * cols)
        for n in range(dc // 256):
            c = slice(n * 256, (n + 1) * 256)
            piece = lax.dot_general(
                delta, wbuf[c, :], (((1,), (1,)), ((), ())), preferred_element_type=F32
            )
            for g in range(8):
                for q in range(2):
                    r = g * 16 + q * 8
                    pbuf[2 * pair + q, g * 8 : g * 8 + 8, c] = piece[r : r + 8]

    def ring(side, r, dest, limit, device):
        zacc[...] = pbuf[dest]

        @pl.when(r > 0)
        def _():
            take(zr.at[side, r - 1], z_recv.at[side, r - 1])
            zacc[...] += zr[side, r - 1].astype(F32)

        @pl.when(r - 1 >= limit)
        def _():
            take(zrl.at[side, r - 1 - limit], zl_recv.at[side, r - 1 - limit])
            zacc[...] += zrl[side, r - 1 - limit].astype(F32)

        total = zacc[...]
        top = total.astype(BF16)
        zs[side, r] = top
        send(zs.at[side, r], zr.at[side, r], z_send.at[side, r], z_recv.at[side, r], device)

        @pl.when(r >= limit)
        def _():
            zsl[side, r - limit] = (total - top.astype(F32)).astype(BF16)
            send(
                zsl.at[side, r - limit], zrl.at[side, r - limit],
                zl_send.at[side, r - limit], zl_recv.at[side, r - limit], device,
            )

    def reduce_z(r):
        ring(0, r, lax.rem(z + NZ - 8 + r, NZ), 8 - LOW, down_z)

        @pl.when(r < 7)
        def _():
            ring(1, r, lax.rem(z + 7 - r, NZ), 7 - LOW, up_z)

    def end_z():
        total = pbuf[z]
        for side, last in ((0, 7), (1, 6)):
            take(zr.at[side, last], z_recv.at[side, last])
            total += zr[side, last].astype(F32)
            if LOW:
                take(zrl.at[side, LOW - 1], zl_recv.at[side, LOW - 1])
                total += zrl[side, LOW - 1].astype(F32)
        for g in range(8):
            a, b = total[g * 8 : g * 8 + 4], total[g * 8 + 4 : g * 8 + 8]
            fown[g * 4 : g * 4 + 4] = jnp.where(xh == 0, a, b)
            fs[g * 4 : g * 4 + 4] = jnp.where(xh == 0, b, a)
        send(fs, fr, f_send, f_recv, over_h)

    def end_h():
        take(fr, f_recv)
        total = fown[...] + fr[...]
        for g in range(8):
            ps[g] = total[g * 4 : g * 4 + 4].astype(BF16)
        for j in range(1, 8):
            g = lax.rem(p + j, 8)
            send(ps.at[g], pr.at[p], p_send.at[j], p_recv.at[j], (g * 2 + core, tensor))
        pr[p] = ps[p]

    def weight_tile(w):
        owner = jnp.where(w < 2, 1 - core, core)
        q = lax.rem(w, 2)
        rows = pl.ds(pl.multiple_of(owner * half + q * 256, 256), 256)
        x = xpt[rows, :]
        for n in range(n_w):
            c = slice(n * 256, (n + 1) * 256)
            part = jnp.dot(x, dbuf[:, :, :, :, c].reshape(NS * 128, 256), preferred_element_type=F32)

            @pl.when(w < 2)
            def _():
                ws[q, :, c] = part.astype(BF16)

            @pl.when(w >= 2)
            def _():
                wown[q, :, c] = part

        @pl.when(w < 2)
        def _():
            send(ws.at[q], wr.at[q], ww_send.at[q], ww_recv.at[q], over_c)

    def when(lo, hi, t, body):
        @pl.when(jnp.logical_and(t >= lo, t < hi))
        def _():
            body(t - lo)

    start2 = 10 - FIRST

    def step(t, carry):
        when(0, 8, t, gather_z)
        when(0, 8, t, forward)
        when(1, 9, t, reduce_b)
        when(2, 10, t, reduce_c)
        when(3, 11, t, reduce_d)
        when(start2, start2 + 8, t, lambda i: spread_a(order(i)))
        when(start2 + 1, start2 + 9, t, lambda i: spread_b(order(i)))
        when(start2 + 2, start2 + 10, t, lambda i: spread_c(order(i)))
        when(start2 + 3, start2 + 11, t, lambda i: spread_d(order(i)))
        when(14, 22, t, reduce_z)
        when(22, 23, t, lambda i: end_z())
        when(23, 24, t, lambda i: end_h())
        when(20, 24, t, weight_tile)
        return carry

    lax.fori_loop(0, 24, step, 0)

    for q in range(2):
        take(wr.at[q], ww_recv.at[q])
        rows = slice(q * 256, (q + 1) * 256)
        gg_ref[rows, :] = (wown[q, :, :cols] + wr[q, :, :cols].astype(F32)).astype(BF16)
        ug_ref[rows, :] = (wown[q, :, cols:] + wr[q, :, cols:].astype(F32)).astype(BF16)
    for j in range(1, 8):
        take(pr.at[lax.rem(p + 8 - j, 8)], p_recv.at[j])
    for g in range(8):
        tg_ref[:, g * dc : (g + 1) * dc] = pr[g]

    for j in range(1, 8):
        take(ts.at[0], t_send.at[j])
        take(ps.at[0], p_send.at[j])
    for m, c in enumerate((gate_c, up_c)):
        take(wbuf.at[mine, c], w_send.at[m])
    take(ta, h_send)
    take(fs, f_send)
    for q in range(2):
        take(ws.at[q], ww_send.at[q])

    def drain(s, carry):
        take(xbuf.at[0], az_send.at[0, s])
        take(zs.at[0, s], z_send.at[0, s])

        @pl.when(s < 7)
        def _():
            take(xbuf.at[0], az_send.at[1, s])
            take(zs.at[1, s], z_send.at[1, s])

        for kind, ref in (
            (0, gya.at[s, 0]), (1, gya.at[s, 0]), (2, ux.at[s]), (3, gyb.at[s, 0]), (4, gyb.at[s, 0]),
            (5, uya0.at[s]), (6, uya1.at[s]), (7, gxs.at[s]), (8, us.at[s, 0]), (9, us.at[s, 0]),
            (10, gxs.at[s]), (11, gxs.at[s]), (12, gxs.at[s]), (13, gyb.at[s, 0]), (14, gyb.at[s, 0]),
            (15, uya0.at[s]), (16, uya1.at[s]), (17, gxs.at[s]), (18, gxs.at[s]), (19, ux.at[s]),
        ):
            take(ref, ssem.at[kind, s])
        return carry

    lax.fori_loop(0, NS, drain, 0)
    for side in range(2):
        for s in range(LOW):
            take(zsl.at[side, s], zl_send.at[side, s])


def per_device(tokens, gate_weight, up_weight, hidden_grad):
    half, cols = gate_weight.shape
    rows = tokens.shape[0]
    dc = 2 * half
    group = hidden_grad.shape[0]
    v = pltpu.VMEM
    dma = pltpu.SemaphoreType.DMA
    scratch = [
        v((dc, 2 * cols), BF16),
        v((8, rows, dc), BF16), v((8, rows, dc), BF16), v((8, rows, dc), BF16),
        v((64, dc), F32),
        v((NZ, 64, dc), BF16),
        v((dc, NS * 128), BF16),
        v((NS, 2, 4, 16, 2 * cols), BF16),
        v((4, 2, 4, 16, 2 * cols), F32),
        v((NS, 2, 16, cols), BF16),
        v((NS, 4, 16, cols), BF16),
        v((NS, 2, 2, 16, cols), BF16),
        v((NS, 16, cols), BF16), v((NS, 16, cols), BF16),
        v((4, 16, cols), F32),
        v((4, 4, 16, cols), F32),
        v((NS, 4, 16, cols), BF16),
        v((NS, 16, CUT), BF16), v((NS, 16, cols - CUT), BF16),
        v((NS, 2, 16, cols), BF16),
        v((NS, 2, 4, 16, 2 * cols), BF16),
        v((NZ, 64, dc), F32),
        v((64, dc), F32),
        v((2, 8, 64, dc), BF16), v((2, 8, 64, dc), BF16),
        v((2, LOW, 64, dc), BF16), v((2, LOW, 64, dc), BF16),
        v((32, dc), F32), v((32, dc), F32), v((32, dc), F32),
        v((8, rows, dc), BF16), v((8, rows, dc), BF16),
        v((2, 256, 2 * cols), BF16), v((2, 256, 2 * cols), BF16),
        v((2, 256, 2 * cols), F32),
        dma((2,)), dma((2,)), dma((2,)),
        dma((8,)), dma((8,)),
        dma, dma,
        dma((2, 8)), dma((2, 8)),
        dma((20, NS)), dma((20, NS)),
        dma((2, 8)), dma((2, 8)),
        dma((2, LOW)), dma((2, LOW)),
        dma, dma,
        dma((8,)), dma((8,)),
        dma((2,)), dma((2,)),
    ]
    vm = pl.BlockSpec(memory_space=pltpu.VMEM)
    hbm = pl.BlockSpec(memory_space=pl.ANY)
    return pl.pallas_call(
        kernel,
        out_shape=(
            jax.ShapeDtypeStruct((group, cols), BF16),
            jax.ShapeDtypeStruct(tokens.shape, BF16),
            jax.ShapeDtypeStruct((half, cols), BF16),
            jax.ShapeDtypeStruct((half, cols), BF16),
        ),
        in_specs=[vm, hbm, hbm, vm],
        out_specs=(vm, vm, vm, vm),
        scratch_shapes=scratch,
        compiler_params=pltpu.CompilerParams(
            collective_id=0, has_side_effects=True, vmem_limit_bytes=60 * 1024 * 1024
        ),
        cost_estimate=pl.CostEstimate(flops=11_300_000_000, bytes_accessed=6_000_000, transcendentals=114_688),
    )(tokens, gate_weight, up_weight, hidden_grad)


def solution(mesh):
    placed = (P(("dp", "tensor"), None), P("dp", "tensor"), P("dp", "tensor"), P("dp", "tensor"))
    return jax.shard_map(
        per_device,
        mesh=mesh,
        in_specs=placed,
        out_specs=(
            P("dp", "tensor"),
            P(("dp", "tensor"), None),
            P("dp", "tensor"),
            P("dp", "tensor"),
        ),
        check_vma=False,
    )
```

```python
import functools

import jax
import jax.numpy as jnp
from jax import lax
from jax.experimental import pallas as pl
from jax.experimental.pallas import tpu as pltpu
from jax.sharding import PartitionSpec as P

MESH = pl.DeviceIdType.MESH
F32 = jnp.float32
BF16 = jnp.bfloat16
NZ = 16
NS = 8
CY = 768
FIRST = 2
LOW = 2
NU = 4
SUB = 16


def send(src, dst, send_sem, recv_sem, device):
    pltpu.make_async_remote_copy(
        src_ref=src,
        dst_ref=dst,
        send_sem=send_sem,
        recv_sem=recv_sem,
        device_id=device,
        device_id_type=MESH,
    ).start()


def take(ref, sem):
    pltpu.make_async_copy(ref, ref, sem).wait()


def kernel(
    tok_ref, gw_ref, uw_ref, hg_ref,
    hid_ref, tg_ref, gg_ref, ug_ref,
    wbuf, ts, ta, asm, xbuf, xcur, xpt, hgb, hidb,
    sbuf, fbuf, gyb, gxs, gxr, gown, ux, uacc, us, uyb,
    dbuf, pbuf, zacc, zs, zr, zsl, zrl,
    fs, fr, ws, wr, wown, wout,
    l_sem, w_send, w_recv, t_send, t_recv, az_send, az_recv,
    ssem, rsem, z_send, z_recv, zl_send, zl_recv, f_send, f_recv, ww_send, ww_recv, o_sem,
):
    dp, tensor = lax.axis_index("dp"), lax.axis_index("tensor")
    core = lax.rem(dp, 2)
    p = dp // 2
    y, xl = lax.rem(p, 4), p // 4
    xh, z = lax.rem(tensor, 2), tensor // 2
    xo = 1 - xl

    def row_of(k):
        return lax.rem(y + k, 4)

    def at_y(k):
        return ((xl * 4 + row_of(k)) * 2 + core, tensor)

    over_x = ((xo * 4 + y) * 2 + core, tensor)
    up_z = (dp, lax.rem(z + 1, NZ) * 2 + xh)
    down_z = (dp, lax.rem(z + NZ - 1, NZ) * 2 + xh)
    over_c = (p * 2 + (1 - core), tensor)
    plane = [(j, h) for h in range(2) for j in range(8) if j or h]

    def to_plane(j, h):
        g, hh = lax.rem(p + j, 8), lax.rem(xh + h, 2)
        return g, hh, (g * 2 + core, z * 2 + hh)

    half = gw_ref.shape[0]
    cols = gw_ref.shape[1]
    dc = 2 * half
    wide = 2 * cols
    gate_c, up_c = pl.ds(0, cols), pl.ds(cols, cols)
    y_c, x_c = pl.ds(0, CY), pl.ds(CY, wide - CY)

    barrier = pltpu.get_barrier_semaphore()
    for j, h in plane:
        pl.semaphore_signal(barrier, inc=1, device_id=to_plane(j, h)[2], device_id_type=MESH)
    for other in (up_z, down_z, over_c):
        pl.semaphore_signal(barrier, inc=1, device_id=other, device_id_type=MESH)
    mine = pl.ds(pl.multiple_of(core * half, half), half)
    theirs = pl.ds(pl.multiple_of((1 - core) * half, half), half)
    for m, (w_ref, c) in enumerate(((gw_ref, gate_c), (uw_ref, up_c))):
        pltpu.make_async_copy(w_ref, wbuf.at[mine, c], l_sem.at[m]).start()
    pltpu.make_async_copy(hg_ref, hgb, l_sem.at[2]).start()
    for g in range(8):
        ts[g] = tok_ref[:, g * dc : (g + 1) * dc]
    pl.semaphore_wait(barrier, 18)

    for j, h in plane:
        g, hh, device = to_plane(j, h)
        send(ts.at[g], ta.at[xh, p], t_send.at[h, j], t_recv.at[h, j], device)
    for m, (w_ref, c) in enumerate(((gw_ref, gate_c), (uw_ref, up_c))):
        send(w_ref, wbuf.at[mine, c], w_send.at[m], w_recv.at[m], over_c)
    ta[xh, p] = ts[p]
    for j, h in plane:
        take(ta.at[lax.rem(xh + h, 2), lax.rem(p + 8 - j, 8)], t_recv.at[h, j])
    for g in range(8):
        asm[g * 8 : g * 8 + 4] = ta[0, g].astype(F32)
        asm[g * 8 + 4 : g * 8 + 8] = ta[1, g].astype(F32)
    xbuf[z] = asm[...].astype(BF16)

    def block(b, u):
        return xbuf.at[b, pl.ds(u * SUB, SUB), :]

    def send_block(side, b, u, s):
        device = up_z if side == 0 else down_z
        send(block(b, u), block(b, u), az_send.at[side, s, u], az_recv.at[side, s, u], device)

    for u in range(NU):
        send_block(0, z, u, 0)
        send_block(1, z, u, 0)

    for m, c in enumerate((gate_c, up_c)):
        take(wbuf.at[mine, c], l_sem.at[m])
        take(wbuf.at[theirs, c], w_recv.at[m])
    take(hgb, l_sem.at[2])

    def pair_of(s):
        hop = (s + 1) // 2
        sign = 1 - 2 * lax.rem(s + z, 2)
        return lax.rem(z // 2 + sign * hop + NS, NS)

    def gather_z(s, part):
        lo = lax.rem(z + NZ - 1 - s, NZ)
        hi = lax.rem(z + 1 + s, NZ)
        for u in part:
            take(block(lo, u), az_recv.at[0, s, u])

            @pl.when(s < 7)
            def _():
                send_block(0, lo, u, s + 1)
                take(block(hi, u), az_recv.at[1, s, u])

            @pl.when(s < 6)
            def _():
                send_block(1, hi, u, s + 1)

    def rows_of(s):
        pair = pair_of(s)
        x0 = xbuf[2 * pair].astype(F32)
        x1 = xbuf[2 * pair + 1].astype(F32)
        rows = []
        for g in range(8):
            rows += [x0[g * 8 : g * 8 + 8], x1[g * 8 : g * 8 + 8]]
        return jnp.concatenate(rows, axis=0)

    def forward(s, part):
        slot = lax.rem(s, 4)
        if part == 0:
            xp = rows_of(s).astype(BF16)
            xcur[...] = xp
            blocks = range(CY // 256, wide // 256)
        else:
            xp = xcur[...]
            blocks = range(CY // 256)
        for n in blocks:
            c = slice(n * 256, (n + 1) * 256)
            part_sum = jnp.dot(xp, wbuf[:, c], preferred_element_type=F32).reshape(2, 4, 16, 256)
            fbuf[slot, :, :, :, c] = part_sum
            sbuf[s, :, :, :, c] = part_sum.astype(BF16)
        if part == 0:
            send(sbuf.at[s, xo, :, :, x_c], ux.at[s], ssem.at[3, s], rsem.at[3, s], over_x)
        else:
            for k in (1, 2, 3):
                send(
                    sbuf.at[s, :, row_of(k), :, y_c], gyb.at[s, k - 1],
                    ssem.at[k - 1, s], rsem.at[k - 1, s], at_y(k),
                )

    def reduce_b(s):
        slot = lax.rem(s, 4)
        take(ux.at[s], rsem.at[3, s])
        total = fbuf[slot, xl, :, :, CY:] + ux[s].astype(F32)
        uacc[slot] = total
        us[s] = total.astype(BF16)
        for k in (1, 2, 3):
            send(us.at[s, row_of(k)], uyb.at[s, k - 1], ssem.at[4 + k, s], rsem.at[4 + k, s], at_y(k))
        for k in (1, 2, 3):
            take(gyb.at[s, k - 1], rsem.at[k - 1, s])

        def side(xx):
            total = fbuf[slot, xx, y, :, :CY]
            for k in range(3):
                total += gyb[s, k, xx].astype(F32)
            return total

        gxs[s] = side(xo).astype(BF16)
        send(gxs.at[s], gxr.at[s], ssem.at[4, s], rsem.at[4, s], over_x)
        gown[slot] = side(xl)

    def reduce_c(s):
        slot = lax.rem(s, 4)
        rows = pl.ds(pl.multiple_of(pair_of(s) * 16, 16), 16)
        for k in (1, 2, 3):
            take(uyb.at[s, k - 1], rsem.at[4 + k, s])
        take(gxr.at[s], rsem.at[4, s])
        first = gown[slot] + gxr[s].astype(F32)
        second = uacc[slot, y]
        for k in range(3):
            second += uyb[s, k].astype(F32)
        full = jnp.concatenate([first, second], axis=1)
        gate, up = full[:, :cols], full[:, cols:]
        sig = jax.nn.sigmoid(gate)
        act = gate * sig
        hidb[rows, :] = (act * up).astype(BF16)
        cot = hgb[rows, :].astype(F32)
        dbuf[s, xl, y, :, :cols] = (cot * up * sig * (1.0 + gate * (1.0 - sig))).astype(BF16)
        dbuf[s, xl, y, :, cols:] = (cot * act).astype(BF16)

    def order(i):
        return jnp.where(i < FIRST, i, NS - 1 + FIRST - i)

    def same(ref, kind, s, device):
        send(ref, ref, ssem.at[kind, s], rsem.at[kind, s], device)

    def spread_a(s):
        for k in (1, 2, 3):
            same(dbuf.at[s, xl, y, :, x_c], 8 + k, s, at_y(k))
        same(dbuf.at[s, xl, y, :, y_c], 8, s, over_x)

    def spread_b(s):
        take(dbuf.at[s, xo, y, :, y_c], rsem.at[8, s])
        for k in (1, 2, 3):
            same(dbuf.at[s, :, y, :, y_c], 11 + k, s, at_y(k))
        for k in (1, 2, 3):
            take(dbuf.at[s, xl, row_of(4 - k), :, x_c], rsem.at[8 + k, s])
        same(dbuf.at[s, xl, :, :, x_c], 15, s, over_x)

    def spread_c(s, part):
        if part == 0:
            for k in (1, 2, 3):
                take(dbuf.at[s, :, row_of(4 - k), :, y_c], rsem.at[11 + k, s])
            take(dbuf.at[s, xo, :, :, x_c], rsem.at[15, s])
        pair = pair_of(s)
        delta = dbuf[s].reshape(128, wide)
        width = dc // 2
        for n in range(part * width // 256, (part + 1) * width // 256):
            c = slice(n * 256, (n + 1) * 256)
            piece = lax.dot_general(
                delta, wbuf[c, :], (((1,), (1,)), ((), ())), preferred_element_type=F32
            )
            for g in range(8):
                for q in range(2):
                    r = g * 16 + q * 8
                    pbuf[2 * pair + q, g * 8 : g * 8 + 8, c] = piece[r : r + 8]

    def ring(side, r, u):
        dest = lax.rem(z + NZ - 8 + r, NZ) if side == 0 else lax.rem(z + 7 - r, NZ)
        limit = (8 if side == 0 else 7) - LOW
        device = down_z if side == 0 else up_z
        rows = pl.ds(u * SUB, SUB)
        zacc[...] = pbuf[dest, rows, :]

        @pl.when(r > 0)
        def _():
            take(zr.at[side, r - 1, rows], z_recv.at[side, r - 1, u])
            zacc[...] += zr[side, r - 1, rows].astype(F32)

        @pl.when(r - 1 >= limit)
        def _():
            take(zrl.at[side, r - 1 - limit, rows], zl_recv.at[side, r - 1 - limit, u])
            zacc[...] += zrl[side, r - 1 - limit, rows].astype(F32)

        total = zacc[...]
        top = total.astype(BF16)
        zs[side, r, rows] = top
        send(zs.at[side, r, rows], zr.at[side, r, rows], z_send.at[side, r, u], z_recv.at[side, r, u], device)

        @pl.when(r >= limit)
        def _():
            zsl[side, r - limit, rows] = (total - top.astype(F32)).astype(BF16)
            send(
                zsl.at[side, r - limit, rows], zrl.at[side, r - limit, rows],
                zl_send.at[side, r - limit, u], zl_recv.at[side, r - limit, u], device,
            )

    def reduce_z(r, part):
        for u in part:
            ring(0, r, u)

            @pl.when(r > 0)
            def _():
                ring(1, r - 1, u)

    def end_z():
        for u in range(NU):
            rows = pl.ds(u * SUB, SUB)
            total = pbuf[z, rows, :]
            for side, last in ((0, 7), (1, 6)):
                take(zr.at[side, last, rows], z_recv.at[side, last, u])
                total += zr[side, last, rows].astype(F32)
                take(zrl.at[side, LOW - 1, rows], zl_recv.at[side, LOW - 1, u])
                total += zrl[side, LOW - 1, rows].astype(F32)
            for i in range(SUB // 8):
                g = u * (SUB // 8) + i
                fs[0, g] = total[i * 8 : i * 8 + 4]
                fs[1, g] = total[i * 8 + 4 : i * 8 + 8]
        for j, h in plane:
            g, hh, device = to_plane(j, h)
            send(fs.at[hh, g], fr.at[xh, p], f_send.at[h, j], f_recv.at[h, j], device)
        fr[xh, p] = fs[xh, p]

    def turn(s):
        xpt[:, pl.ds(pl.multiple_of(s * 128, 128), 128)] = rows_of(s).T.astype(BF16)

    def weight_tile(w, part):
        owner = jnp.where(w < 2, 1 - core, core)
        q = lax.rem(w, 2)
        rows = pl.ds(pl.multiple_of(owner * half + q * 256, 256), 256)
        x = xpt[rows, :]
        for n in range(4) if part == 0 else range(4, wide // 256):
            c = slice(n * 256, (n + 1) * 256)
            total = jnp.dot(x, dbuf[:, :, :, :, c].reshape(NS * 128, 256), preferred_element_type=F32)

            @pl.when(w < 2)
            def _():
                ws[q, :, c] = total.astype(BF16)

            @pl.when(w >= 2)
            def _():
                wown[q, :, c] = total

        if part == 1:

            @pl.when(w < 2)
            def _():
                send(ws.at[q], wr.at[q], ww_send.at[q], ww_recv.at[q], over_c)

    def when(lo, hi, t, body):
        @pl.when(jnp.logical_and(t >= lo, t < hi))
        def _():
            body(t - lo)

    start2 = 12 - FIRST

    def gather_at(t, u):
        when(0, 8, t, lambda s: gather_z(s, range(u, u + 1)))

    def ring_at(t, u):
        when(15, 23, t, lambda r: reduce_z(r, range(u, u + 1)))

    def step(t, carry):
        ring_at(t, 0)
        gather_at(t, 0)
        when(5, 13, t, reduce_c)
        when(start2, start2 + 8, t, lambda i: spread_a(order(i)))
        gather_at(t, 1)
        when(3, 11, t, reduce_b)
        when(start2 + 1, start2 + 9, t, lambda i: spread_b(order(i)))
        ring_at(t, 1)
        gather_at(t, 2)
        when(1, 9, t, lambda s: forward(s, 0))
        when(start2 + 2, start2 + 10, t, lambda i: spread_c(order(i), 0))
        when(20, 24, t, lambda w: weight_tile(w, 0))
        ring_at(t, 2)
        gather_at(t, 3)
        when(1, 9, t, lambda s: forward(s, 1))
        when(start2 + 2, start2 + 10, t, lambda i: spread_c(order(i), 1))
        ring_at(t, 3)
        when(23, 24, t, lambda i: end_z())
        when(20, 24, t, lambda w: weight_tile(w, 1))
        when(8, 16, t, turn)
        return carry

    lax.fori_loop(0, 24, step, 0)

    pltpu.make_async_copy(hidb, hid_ref, o_sem.at[0]).start()
    for q in range(2):
        take(wr.at[q], ww_recv.at[q])
        wout[q] = (wown[q] + wr[q].astype(F32)).astype(BF16)
        rows = pl.ds(q * 256, 256)
        pltpu.make_async_copy(wout.at[q, :, gate_c], gg_ref.at[rows, :], o_sem.at[1 + q]).start()
        pltpu.make_async_copy(wout.at[q, :, up_c], ug_ref.at[rows, :], o_sem.at[3 + q]).start()
    for j, h in plane:
        take(fr.at[lax.rem(xh + h, 2), lax.rem(p + 8 - j, 8)], f_recv.at[h, j])
    for g in range(8):
        tg_ref[:, g * dc : (g + 1) * dc] = (fr[0, g] + fr[1, g]).astype(BF16)

    for j, h in plane:
        take(ts.at[0], t_send.at[h, j])
        take(fs.at[0, 0], f_send.at[h, j])
    for m, c in enumerate((gate_c, up_c)):
        take(wbuf.at[mine, c], w_send.at[m])
    for q in range(2):
        take(ws.at[q], ww_send.at[q])

    def drain(s, carry):
        for u in range(NU):
            take(block(0, u), az_send.at[0, s, u])
            take(zs.at[0, s, pl.ds(u * SUB, SUB)], z_send.at[0, s, u])

            @pl.when(s < 7)
            def _():
                take(block(0, u), az_send.at[1, s, u])
                take(zs.at[1, s, pl.ds(u * SUB, SUB)], z_send.at[1, s, u])

            @pl.when(s < LOW)
            def _():
                for side in range(2):
                    take(zsl.at[side, s, pl.ds(u * SUB, SUB)], zl_send.at[side, s, u])

        for k in range(3):
            take(gyb.at[s, k], ssem.at[k, s])
            take(uyb.at[s, k], ssem.at[5 + k, s])
            take(uyb.at[s, k], ssem.at[9 + k, s])
            take(gyb.at[s, k], ssem.at[12 + k, s])
        take(ux.at[s], ssem.at[3, s])
        take(gxs.at[s], ssem.at[4, s])
        take(gxs.at[s], ssem.at[8, s])
        take(ux.at[s], ssem.at[15, s])
        return carry

    lax.fori_loop(0, NS, drain, 0)
    take(hidb, o_sem.at[0])
    for q in range(2):
        take(wout.at[q, :, gate_c], o_sem.at[1 + q])
        take(wout.at[q, :, up_c], o_sem.at[3 + q])


def per_device(tokens, gate_weight, up_weight, hidden_grad):
    half, cols = gate_weight.shape
    rows = tokens.shape[0]
    dc = 2 * half
    wide = 2 * cols
    cx = wide - CY
    group = hidden_grad.shape[0]
    v = pltpu.VMEM
    dma = pltpu.SemaphoreType.DMA
    scratch = [
        v((dc, wide), BF16),
        v((8, rows, dc), BF16), v((2, 8, rows, dc), BF16),
        v((64, dc), F32),
        v((NZ, 64, dc), BF16),
        v((128, dc), BF16),
        v((dc, NS * 128), BF16),
        v((group, cols), BF16), v((group, cols), BF16),
        v((NS, 2, 4, 16, wide), BF16),
        v((4, 2, 4, 16, wide), F32),
        v((NS, 3, 2, 16, CY), BF16),
        v((NS, 16, CY), BF16), v((NS, 16, CY), BF16),
        v((4, 16, CY), F32),
        v((NS, 4, 16, cx), BF16),
        v((4, 4, 16, cx), F32),
        v((NS, 4, 16, cx), BF16),
        v((NS, 3, 16, cx), BF16),
        v((NS, 2, 4, 16, wide), BF16),
        v((NZ, 64, dc), F32),
        v((SUB, dc), F32),
        v((2, 8, 64, dc), BF16), v((2, 8, 64, dc), BF16),
        v((2, LOW, 64, dc), BF16), v((2, LOW, 64, dc), BF16),
        v((2, 8, rows, dc), F32), v((2, 8, rows, dc), F32),
        v((2, 256, wide), BF16), v((2, 256, wide), BF16),
        v((2, 256, wide), F32),
        v((2, 256, wide), BF16),
        dma((3,)), dma((2,)), dma((2,)),
        dma((2, 8)), dma((2, 8)),
        dma((2, 8, NU)), dma((2, 8, NU)),
        dma((16, NS)), dma((16, NS)),
        dma((2, 8, NU)), dma((2, 8, NU)),
        dma((2, LOW, NU)), dma((2, LOW, NU)),
        dma((2, 8)), dma((2, 8)),
        dma((2,)), dma((2,)),
        dma((5,)),
    ]
    vm = pl.BlockSpec(memory_space=pltpu.VMEM)
    hbm = pl.BlockSpec(memory_space=pl.ANY)
    return pl.pallas_call(
        kernel,
        out_shape=(
            jax.ShapeDtypeStruct((group, cols), BF16),
            jax.ShapeDtypeStruct(tokens.shape, BF16),
            jax.ShapeDtypeStruct((half, cols), BF16),
            jax.ShapeDtypeStruct((half, cols), BF16),
        ),
        in_specs=[vm, hbm, hbm, hbm],
        out_specs=(hbm, vm, hbm, hbm),
        scratch_shapes=scratch,
        compiler_params=pltpu.CompilerParams(
            collective_id=0, has_side_effects=True, vmem_limit_bytes=60 * 1024 * 1024
        ),
        cost_estimate=pl.CostEstimate(flops=11_300_000_000, bytes_accessed=6_000_000, transcendentals=114_688),
    )(tokens, gate_weight, up_weight, hidden_grad)


def solution(mesh):
    placed = (P(("dp", "tensor"), None), P("dp", "tensor"), P("dp", "tensor"), P("dp", "tensor"))
    return jax.shard_map(
        per_device,
        mesh=mesh,
        in_specs=placed,
        out_specs=(
            P("dp", "tensor"),
            P(("dp", "tensor"), None),
            P("dp", "tensor"),
            P("dp", "tensor"),
        ),
        check_vma=False,
    )
```

```python
import functools

import jax
import jax.numpy as jnp
from jax import lax
from jax.experimental import pallas as pl
from jax.experimental.pallas import tpu as pltpu
from jax.sharding import PartitionSpec as P

MESH = pl.DeviceIdType.MESH
F32 = jnp.float32
BF16 = jnp.bfloat16
NZ = 16
NS = 8
CY = 768
FIRST = 0
LOW = 2
NU = 4
SUB = 16


def send(src, dst, send_sem, recv_sem, device):
    pltpu.make_async_remote_copy(
        src_ref=src,
        dst_ref=dst,
        send_sem=send_sem,
        recv_sem=recv_sem,
        device_id=device,
        device_id_type=MESH,
    ).start()


def take(ref, sem):
    pltpu.make_async_copy(ref, ref, sem).wait()


def kernel(
    tok_ref, gw_ref, uw_ref, hg_ref,
    hid_ref, tg_ref, gg_ref, ug_ref,
    wbuf, ts, ta, asm, xbuf, xcur, xpt, hgb, hidb,
    sbuf, fbuf, gyb, gxs, gxr, gown, ux, uacc, us, uyb,
    dbuf, pbuf, zacc, zs, zr, zsl, zrl,
    fs, fr, ws, wr, wown, wout,
    l_sem, w_send, w_recv, t_send, t_recv, az_send, az_recv,
    ssem, rsem, z_send, z_recv, zl_send, zl_recv, f_send, f_recv, ww_send, ww_recv, o_sem,
):
    dp, tensor = lax.axis_index("dp"), lax.axis_index("tensor")
    core = lax.rem(dp, 2)
    p = dp // 2
    y, xl = lax.rem(p, 4), p // 4
    xh, z = lax.rem(tensor, 2), tensor // 2
    xo = 1 - xl

    def row_of(k):
        return lax.rem(y + k, 4)

    def at_y(k):
        return ((xl * 4 + row_of(k)) * 2 + core, tensor)

    over_x = ((xo * 4 + y) * 2 + core, tensor)
    up_z = (dp, lax.rem(z + 1, NZ) * 2 + xh)
    down_z = (dp, lax.rem(z + NZ - 1, NZ) * 2 + xh)
    over_c = (p * 2 + (1 - core), tensor)
    plane = [(j, h) for h in range(2) for j in range(8) if j or h]

    def to_plane(j, h):
        g, hh = lax.rem(p + j, 8), lax.rem(xh + h, 2)
        return g, hh, (g * 2 + core, z * 2 + hh)

    half = gw_ref.shape[0]
    cols = gw_ref.shape[1]
    dc = 2 * half
    wide = 2 * cols
    gate_c, up_c = pl.ds(0, cols), pl.ds(cols, cols)
    y_c, x_c = pl.ds(0, CY), pl.ds(CY, wide - CY)

    barrier = pltpu.get_barrier_semaphore()
    for j, h in plane:
        pl.semaphore_signal(barrier, inc=1, device_id=to_plane(j, h)[2], device_id_type=MESH)
    for other in (up_z, down_z, over_c):
        pl.semaphore_signal(barrier, inc=1, device_id=other, device_id_type=MESH)
    mine = pl.ds(pl.multiple_of(core * half, half), half)
    theirs = pl.ds(pl.multiple_of((1 - core) * half, half), half)
    for m, (w_ref, c) in enumerate(((gw_ref, gate_c), (uw_ref, up_c))):
        pltpu.make_async_copy(w_ref, wbuf.at[mine, c], l_sem.at[m]).start()
    pltpu.make_async_copy(hg_ref, hgb, l_sem.at[2]).start()
    for g in range(8):
        ts[g] = tok_ref[:, g * dc : (g + 1) * dc]
    pl.semaphore_wait(barrier, 18)

    for j, h in plane:
        g, hh, device = to_plane(j, h)
        send(ts.at[g], ta.at[xh, p], t_send.at[h, j], t_recv.at[h, j], device)
    ta[xh, p] = ts[p]
    for m, c in enumerate((gate_c, up_c)):
        take(wbuf.at[mine, c], l_sem.at[m])
        send(wbuf.at[mine, c], wbuf.at[mine, c], w_send.at[m], w_recv.at[m], over_c)
    for j, h in plane:
        take(ta.at[lax.rem(xh + h, 2), lax.rem(p + 8 - j, 8)], t_recv.at[h, j])
    for g in range(8):
        asm[g * 8 : g * 8 + 4] = ta[0, g].astype(F32)
        asm[g * 8 + 4 : g * 8 + 8] = ta[1, g].astype(F32)
    xbuf[z] = asm[...].astype(BF16)

    def block(b, u):
        return xbuf.at[b, pl.ds(u * SUB, SUB), :]

    def send_block(side, b, u, s):
        device = up_z if side == 0 else down_z
        send(block(b, u), block(b, u), az_send.at[side, s, u], az_recv.at[side, s, u], device)

    for u in range(NU):
        send_block(0, z, u, 0)
        send_block(1, z, u, 0)


    def pair_of(s):
        hop = (s + 1) // 2
        sign = 1 - 2 * lax.rem(s + z, 2)
        return lax.rem(z // 2 + sign * hop + NS, NS)

    def gather_z(s, part):
        lo = lax.rem(z + NZ - 1 - s, NZ)
        hi = lax.rem(z + 1 + s, NZ)
        for u in part:
            take(block(lo, u), az_recv.at[0, s, u])

            @pl.when(s < 7)
            def _():
                send_block(0, lo, u, s + 1)
                take(block(hi, u), az_recv.at[1, s, u])

            @pl.when(s < 6)
            def _():
                send_block(1, hi, u, s + 1)

    def rows_of(s):
        pair = pair_of(s)
        x0 = xbuf[2 * pair].astype(F32)
        x1 = xbuf[2 * pair + 1].astype(F32)
        rows = []
        for g in range(8):
            rows += [x0[g * 8 : g * 8 + 8], x1[g * 8 : g * 8 + 8]]
        return jnp.concatenate(rows, axis=0)

    def forward(s, part):
        slot = lax.rem(s, 4)
        if part == 0:

            @pl.when(s == 0)
            def _():
                for m, c in enumerate((gate_c, up_c)):
                    take(wbuf.at[theirs, c], w_recv.at[m])
                take(hgb, l_sem.at[2])

            xp = rows_of(s).astype(BF16)
            xcur[s] = xp
            blocks = range(CY // 256, wide // 256)
        else:
            xp = xcur[s]
            blocks = range(CY // 256)
        for n in blocks:
            c = slice(n * 256, (n + 1) * 256)
            part_sum = jnp.dot(xp, wbuf[:, c], preferred_element_type=F32).reshape(2, 4, 16, 256)
            fbuf[slot, :, :, :, c] = part_sum
            sbuf[s, :, :, :, c] = part_sum.astype(BF16)
        if part == 0:
            send(sbuf.at[s, xo, :, :, x_c], ux.at[s], ssem.at[3, s], rsem.at[3, s], over_x)
        else:
            for k in (1, 2, 3):
                send(
                    sbuf.at[s, :, row_of(k), :, y_c], gyb.at[s, k - 1],
                    ssem.at[k - 1, s], rsem.at[k - 1, s], at_y(k),
                )

    def reduce_b(s):
        slot = lax.rem(s, 4)
        take(ux.at[s], rsem.at[3, s])
        total = fbuf[slot, xl, :, :, CY:] + ux[s].astype(F32)
        uacc[slot] = total
        us[s] = total.astype(BF16)
        for k in (1, 2, 3):
            send(us.at[s, row_of(k)], uyb.at[s, k - 1], ssem.at[4 + k, s], rsem.at[4 + k, s], at_y(k))
        for k in (1, 2, 3):
            take(gyb.at[s, k - 1], rsem.at[k - 1, s])

        def side(xx):
            total = fbuf[slot, xx, y, :, :CY]
            for k in range(3):
                total += gyb[s, k, xx].astype(F32)
            return total

        gxs[s] = side(xo).astype(BF16)
        send(gxs.at[s], gxr.at[s], ssem.at[4, s], rsem.at[4, s], over_x)
        gown[slot] = side(xl)

    def reduce_c(s):
        slot = lax.rem(s, 4)
        rows = pl.ds(pl.multiple_of(pair_of(s) * 16, 16), 16)
        for k in (1, 2, 3):
            take(uyb.at[s, k - 1], rsem.at[4 + k, s])
        take(gxr.at[s], rsem.at[4, s])
        first = gown[slot] + gxr[s].astype(F32)
        second = uacc[slot, y]
        for k in range(3):
            second += uyb[s, k].astype(F32)
        full = jnp.concatenate([first, second], axis=1)
        gate, up = full[:, :cols], full[:, cols:]
        sig = jax.nn.sigmoid(gate)
        act = gate * sig
        hidb[rows, :] = (act * up).astype(BF16)
        cot = hgb[rows, :].astype(F32)
        dbuf[s, xl, y, :, :cols] = (cot * up * sig * (1.0 + gate * (1.0 - sig))).astype(BF16)
        dbuf[s, xl, y, :, cols:] = (cot * act).astype(BF16)

    def order(i):
        return jnp.where(i < FIRST, i, NS - 1 + FIRST - i)

    def same(ref, kind, s, device):
        send(ref, ref, ssem.at[kind, s], rsem.at[kind, s], device)

    def spread_a(s):
        same(dbuf.at[s, xl, y, :, y_c], 8, s, over_x)
        for k in (1, 2, 3):
            same(dbuf.at[s, xl, y, :, x_c], 8 + k, s, at_y(k))

    def spread_b(s):
        take(dbuf.at[s, xo, y, :, y_c], rsem.at[8, s])
        for k in (1, 2, 3):
            same(dbuf.at[s, :, y, :, y_c], 11 + k, s, at_y(k))
        for k in (1, 2, 3):
            take(dbuf.at[s, xl, row_of(4 - k), :, x_c], rsem.at[8 + k, s])
        same(dbuf.at[s, xl, :, :, x_c], 15, s, over_x)

    def spread_c(s, part):
        if part == 0:
            for k in (1, 2, 3):
                take(dbuf.at[s, :, row_of(4 - k), :, y_c], rsem.at[11 + k, s])
            take(dbuf.at[s, xo, :, :, x_c], rsem.at[15, s])
        pair = pair_of(s)
        delta = dbuf[s].reshape(128, wide)
        width = dc // 2
        for n in range(part * width // 256, (part + 1) * width // 256):
            c = slice(n * 256, (n + 1) * 256)
            piece = lax.dot_general(
                delta, wbuf[c, :], (((1,), (1,)), ((), ())), preferred_element_type=F32
            )
            for g in range(8):
                for q in range(2):
                    r = g * 16 + q * 8
                    pbuf[2 * pair + q, g * 8 : g * 8 + 8, c] = piece[r : r + 8]

    def ring(side, r, u):
        dest = lax.rem(z + NZ - 8 + r, NZ) if side == 0 else lax.rem(z + 7 - r, NZ)
        limit = (8 if side == 0 else 7) - LOW
        device = down_z if side == 0 else up_z
        rows = pl.ds(u * SUB, SUB)
        zacc[...] = pbuf[dest, rows, :]

        @pl.when(r > 0)
        def _():
            take(zr.at[side, r - 1, rows], z_recv.at[side, r - 1, u])
            zacc[...] += zr[side, r - 1, rows].astype(F32)

        @pl.when(r - 1 >= limit)
        def _():
            take(zrl.at[side, r - 1 - limit, rows], zl_recv.at[side, r - 1 - limit, u])
            zacc[...] += zrl[side, r - 1 - limit, rows].astype(F32)

        total = zacc[...]
        top = total.astype(BF16)
        zs[side, r, rows] = top
        send(zs.at[side, r, rows], zr.at[side, r, rows], z_send.at[side, r, u], z_recv.at[side, r, u], device)

        @pl.when(r >= limit)
        def _():
            zsl[side, r - limit, rows] = (total - top.astype(F32)).astype(BF16)
            send(
                zsl.at[side, r - limit, rows], zrl.at[side, r - limit, rows],
                zl_send.at[side, r - limit, u], zl_recv.at[side, r - limit, u], device,
            )

    def reduce_z(r, part):
        for u in part:
            ring(0, r, u)

            @pl.when(r > 0)
            def _():
                ring(1, r - 1, u)

    def end_z():
        for u in range(NU):
            rows = pl.ds(u * SUB, SUB)
            total = pbuf[z, rows, :]
            for side, last in ((0, 7), (1, 6)):
                take(zr.at[side, last, rows], z_recv.at[side, last, u])
                total += zr[side, last, rows].astype(F32)
                take(zrl.at[side, LOW - 1, rows], zl_recv.at[side, LOW - 1, u])
                total += zrl[side, LOW - 1, rows].astype(F32)
            for i in range(SUB // 8):
                g = u * (SUB // 8) + i
                fs[0, g] = total[i * 8 : i * 8 + 4]
                fs[1, g] = total[i * 8 + 4 : i * 8 + 8]
        for j, h in plane:
            g, hh, device = to_plane(j, h)
            send(fs.at[hh, g], fr.at[xh, p], f_send.at[h, j], f_recv.at[h, j], device)
        fr[xh, p] = fs[xh, p]

    def turn(s):
        xpt[:, pl.ds(pl.multiple_of(s * 128, 128), 128)] = xcur[s].T

    def weight_tile(w, part):
        owner = jnp.where(w < 2, 1 - core, core)
        q = lax.rem(w, 2)
        rows = pl.ds(pl.multiple_of(owner * half + q * 256, 256), 256)
        x = xpt[rows, :]
        for n in range(4) if part == 0 else range(4, wide // 256):
            c = slice(n * 256, (n + 1) * 256)
            total = jnp.dot(x, dbuf[:, :, :, :, c].reshape(NS * 128, 256), preferred_element_type=F32)

            @pl.when(w < 2)
            def _():
                ws[q, :, c] = total.astype(BF16)

            @pl.when(w >= 2)
            def _():
                wown[q, :, c] = total

        if part == 1:

            @pl.when(w < 2)
            def _():
                send(ws.at[q], wr.at[q], ww_send.at[q], ww_recv.at[q], over_c)

    def when(lo, hi, t, body):
        @pl.when(jnp.logical_and(t >= lo, t < hi))
        def _():
            body(t - lo)

    start2 = 12 - FIRST

    def gather_at(t, u):
        when(0, 8, t, lambda s: gather_z(s, range(u, u + 1)))

    def ring_at(t, u):
        when(15, 23, t, lambda r: reduce_z(r, range(u, u + 1)))

    def step(t, carry):
        ring_at(t, 0)
        gather_at(t, 0)
        when(5, 13, t, reduce_c)
        when(start2, start2 + 8, t, lambda i: spread_a(order(i)))
        gather_at(t, 1)
        when(3, 11, t, reduce_b)
        when(start2 + 1, start2 + 9, t, lambda i: spread_b(order(i)))
        ring_at(t, 1)
        gather_at(t, 2)
        when(1, 9, t, lambda s: forward(s, 0))
        when(start2 + 2, start2 + 10, t, lambda i: spread_c(order(i), 0))
        when(22 - FIRST, 26 - FIRST, t, lambda w: weight_tile(w, 0))
        ring_at(t, 2)
        gather_at(t, 3)
        when(1, 9, t, lambda s: forward(s, 1))
        when(start2 + 2, start2 + 10, t, lambda i: spread_c(order(i), 1))
        ring_at(t, 3)
        when(23, 24, t, lambda i: end_z())
        when(22 - FIRST, 26 - FIRST, t, lambda w: weight_tile(w, 1))
        when(8, 16, t, turn)
        return carry

    lax.fori_loop(0, max(24, 26 - FIRST), step, 0)

    pltpu.make_async_copy(hidb, hid_ref, o_sem.at[0]).start()
    for q in range(2):
        take(wr.at[q], ww_recv.at[q])
        wout[q] = (wown[q] + wr[q].astype(F32)).astype(BF16)
        rows = pl.ds(q * 256, 256)
        pltpu.make_async_copy(wout.at[q, :, gate_c], gg_ref.at[rows, :], o_sem.at[1 + q]).start()
        pltpu.make_async_copy(wout.at[q, :, up_c], ug_ref.at[rows, :], o_sem.at[3 + q]).start()
    for j, h in plane:
        take(fr.at[lax.rem(xh + h, 2), lax.rem(p + 8 - j, 8)], f_recv.at[h, j])
    for g in range(8):
        tg_ref[:, g * dc : (g + 1) * dc] = (fr[0, g] + fr[1, g]).astype(BF16)

    for j, h in plane:
        take(ts.at[0], t_send.at[h, j])
        take(fs.at[0, 0], f_send.at[h, j])
    for m, c in enumerate((gate_c, up_c)):
        take(wbuf.at[mine, c], w_send.at[m])
    for q in range(2):
        take(ws.at[q], ww_send.at[q])

    def drain(s, carry):
        for u in range(NU):
            take(block(0, u), az_send.at[0, s, u])
            take(zs.at[0, s, pl.ds(u * SUB, SUB)], z_send.at[0, s, u])

            @pl.when(s < 7)
            def _():
                take(block(0, u), az_send.at[1, s, u])
                take(zs.at[1, s, pl.ds(u * SUB, SUB)], z_send.at[1, s, u])

            @pl.when(s < LOW)
            def _():
                for side in range(2):
                    take(zsl.at[side, s, pl.ds(u * SUB, SUB)], zl_send.at[side, s, u])

        for k in range(3):
            take(gyb.at[s, k], ssem.at[k, s])
            take(uyb.at[s, k], ssem.at[5 + k, s])
            take(uyb.at[s, k], ssem.at[9 + k, s])
            take(gyb.at[s, k], ssem.at[12 + k, s])
        take(ux.at[s], ssem.at[3, s])
        take(gxs.at[s], ssem.at[4, s])
        take(gxs.at[s], ssem.at[8, s])
        take(ux.at[s], ssem.at[15, s])
        return carry

    lax.fori_loop(0, NS, drain, 0)
    take(hidb, o_sem.at[0])
    for q in range(2):
        take(wout.at[q, :, gate_c], o_sem.at[1 + q])
        take(wout.at[q, :, up_c], o_sem.at[3 + q])


def finish(*refs):
    for src, dst in zip(refs[:4], refs[4:]):
        dst[...] = src[...]


def per_device(tokens, gate_weight, up_weight, hidden_grad):
    half, cols = gate_weight.shape
    rows = tokens.shape[0]
    dc = 2 * half
    wide = 2 * cols
    cx = wide - CY
    group = hidden_grad.shape[0]
    v = pltpu.VMEM
    dma = pltpu.SemaphoreType.DMA
    scratch = [
        v((dc, wide), BF16),
        v((8, rows, dc), BF16), v((2, 8, rows, dc), BF16),
        v((64, dc), F32),
        v((NZ, 64, dc), BF16),
        v((NS, 128, dc), BF16),
        v((dc, NS * 128), BF16),
        v((group, cols), BF16), v((group, cols), BF16),
        v((NS, 2, 4, 16, wide), BF16),
        v((4, 2, 4, 16, wide), F32),
        v((NS, 3, 2, 16, CY), BF16),
        v((NS, 16, CY), BF16), v((NS, 16, CY), BF16),
        v((4, 16, CY), F32),
        v((NS, 4, 16, cx), BF16),
        v((4, 4, 16, cx), F32),
        v((NS, 4, 16, cx), BF16),
        v((NS, 3, 16, cx), BF16),
        v((NS, 2, 4, 16, wide), BF16),
        v((NZ, 64, dc), F32),
        v((SUB, dc), F32),
        v((2, 8, 64, dc), BF16), v((2, 8, 64, dc), BF16),
        v((2, LOW, 64, dc), BF16), v((2, LOW, 64, dc), BF16),
        v((2, 8, rows, dc), F32), v((2, 8, rows, dc), F32),
        v((2, 256, wide), BF16), v((2, 256, wide), BF16),
        v((2, 256, wide), F32),
        v((2, 256, wide), BF16),
        dma((3,)), dma((2,)), dma((2,)),
        dma((2, 8)), dma((2, 8)),
        dma((2, 8, NU)), dma((2, 8, NU)),
        dma((16, NS)), dma((16, NS)),
        dma((2, 8, NU)), dma((2, 8, NU)),
        dma((2, LOW, NU)), dma((2, LOW, NU)),
        dma((2, 8)), dma((2, 8)),
        dma((2,)), dma((2,)),
        dma((5,)),
    ]
    vm = pl.BlockSpec(memory_space=pltpu.VMEM)
    hbm = pl.BlockSpec(memory_space=pl.ANY)
    shapes = (
        jax.ShapeDtypeStruct((group, cols), BF16),
        jax.ShapeDtypeStruct(tokens.shape, BF16),
        jax.ShapeDtypeStruct((half, cols), BF16),
        jax.ShapeDtypeStruct((half, cols), BF16),
    )
    results = pl.pallas_call(
        kernel,
        out_shape=shapes,
        in_specs=[vm, hbm, hbm, hbm],
        out_specs=(hbm, vm, hbm, hbm),
        scratch_shapes=scratch,
        compiler_params=pltpu.CompilerParams(
            collective_id=0, has_side_effects=True, vmem_limit_bytes=60 * 1024 * 1024
        ),
        cost_estimate=pl.CostEstimate(flops=11_300_000_000, bytes_accessed=6_000_000, transcendentals=114_688),
    )(tokens, gate_weight, up_weight, hidden_grad)
    return pl.pallas_call(
        finish,
        out_shape=shapes,
        in_specs=[vm] * 4,
        out_specs=(vm,) * 4,
    )(*results)


def solution(mesh):
    placed = (P(("dp", "tensor"), None), P("dp", "tensor"), P("dp", "tensor"), P("dp", "tensor"))
    return jax.shard_map(
        per_device,
        mesh=mesh,
        in_specs=placed,
        out_specs=(
            P("dp", "tensor"),
            P(("dp", "tensor"), None),
            P("dp", "tensor"),
            P("dp", "tensor"),
        ),
        check_vma=False,
    )
```

```python
import functools

import jax
import jax.numpy as jnp
from jax import lax
from jax.experimental import pallas as pl
from jax.experimental.pallas import tpu as pltpu
from jax.sharding import PartitionSpec as P

MESH = pl.DeviceIdType.MESH
F32 = jnp.float32
BF16 = jnp.bfloat16
NZ = 16
NS = 8
CY = 768
FIRST = 0
LOW = 2
TURNS = 3
NU = 4
SUB = 16


def send(src, dst, send_sem, recv_sem, device):
    pltpu.make_async_remote_copy(
        src_ref=src,
        dst_ref=dst,
        send_sem=send_sem,
        recv_sem=recv_sem,
        device_id=device,
        device_id_type=MESH,
    ).start()


def take(ref, sem):
    pltpu.make_async_copy(ref, ref, sem).wait()


def kernel(
    tok_ref, gw_ref, uw_ref, hg_ref,
    hid_ref, tg_ref, gg_ref, ug_ref,
    wbuf, wt, ts, ta, asm, xbuf, xcur, xpt, hgb, hidb,
    sbuf, fbuf, gyb, gxs, gxr, gown, ux, uacc, us, uyb,
    dbuf, pbuf, zacc, zs, zr, zsl, zrl,
    fs, fr, ws, wr, wown, wout,
    l_sem, w_send, w_recv, t_send, t_recv, az_send, az_recv,
    ssem, rsem, z_send, z_recv, zl_send, zl_recv, f_send, f_recv, ww_send, ww_recv, o_sem,
):
    dp, tensor = lax.axis_index("dp"), lax.axis_index("tensor")
    core = lax.rem(dp, 2)
    p = dp // 2
    y, xl = lax.rem(p, 4), p // 4
    xh, z = lax.rem(tensor, 2), tensor // 2
    xo = 1 - xl

    def row_of(k):
        return lax.rem(y + k, 4)

    def at_y(k):
        return ((xl * 4 + row_of(k)) * 2 + core, tensor)

    over_x = ((xo * 4 + y) * 2 + core, tensor)
    up_z = (dp, lax.rem(z + 1, NZ) * 2 + xh)
    down_z = (dp, lax.rem(z + NZ - 1, NZ) * 2 + xh)
    over_c = (p * 2 + (1 - core), tensor)
    plane = [(j, h) for h in range(2) for j in range(8) if j or h]

    def to_plane(j, h):
        g, hh = lax.rem(p + j, 8), lax.rem(xh + h, 2)
        return g, hh, (g * 2 + core, z * 2 + hh)

    half = gw_ref.shape[0]
    cols = gw_ref.shape[1]
    dc = 2 * half
    wide = 2 * cols
    gate_c, up_c = pl.ds(0, cols), pl.ds(cols, cols)
    y_c, x_c = pl.ds(0, CY), pl.ds(CY, wide - CY)

    barrier = pltpu.get_barrier_semaphore()
    for j, h in plane:
        pl.semaphore_signal(barrier, inc=1, device_id=to_plane(j, h)[2], device_id_type=MESH)
    for other in (up_z, down_z, over_c):
        pl.semaphore_signal(barrier, inc=1, device_id=other, device_id_type=MESH)
    mine = pl.ds(pl.multiple_of(core * half, half), half)
    theirs = pl.ds(pl.multiple_of((1 - core) * half, half), half)
    for m, (w_ref, c) in enumerate(((gw_ref, gate_c), (uw_ref, up_c))):
        pltpu.make_async_copy(w_ref, wbuf.at[mine, c], l_sem.at[m]).start()
    pltpu.make_async_copy(hg_ref, hgb, l_sem.at[2]).start()
    for g in range(8):
        ts[g] = tok_ref[:, g * dc : (g + 1) * dc]
    pl.semaphore_wait(barrier, 18)

    for j, h in plane:
        g, hh, device = to_plane(j, h)
        send(ts.at[g], ta.at[xh, p], t_send.at[h, j], t_recv.at[h, j], device)
    ta[xh, p] = ts[p]
    for m, c in enumerate((gate_c, up_c)):
        take(wbuf.at[mine, c], l_sem.at[m])
        send(wbuf.at[mine, c], wbuf.at[mine, c], w_send.at[m], w_recv.at[m], over_c)
    for j, h in plane:
        take(ta.at[lax.rem(xh + h, 2), lax.rem(p + 8 - j, 8)], t_recv.at[h, j])
    for g in range(8):
        asm[g * 8 : g * 8 + 4] = ta[0, g].astype(F32)
        asm[g * 8 + 4 : g * 8 + 8] = ta[1, g].astype(F32)
    xbuf[z] = asm[...].astype(BF16)

    def block(b, u):
        return xbuf.at[b, pl.ds(u * SUB, SUB), :]

    def send_block(side, b, u, s):
        device = up_z if side == 0 else down_z
        send(block(b, u), block(b, u), az_send.at[side, s, u], az_recv.at[side, s, u], device)

    for u in range(NU):
        send_block(0, z, u, 0)
        send_block(1, z, u, 0)


    def pair_of(s):
        hop = (s + 1) // 2
        sign = 1 - 2 * lax.rem(s + z, 2)
        return lax.rem(z // 2 + sign * hop + NS, NS)

    def gather_z(s, part):
        lo = lax.rem(z + NZ - 1 - s, NZ)
        hi = lax.rem(z + 1 + s, NZ)
        for u in part:
            take(block(lo, u), az_recv.at[0, s, u])

            @pl.when(s < 7)
            def _():
                send_block(0, lo, u, s + 1)
                take(block(hi, u), az_recv.at[1, s, u])

            @pl.when(s < 6)
            def _():
                send_block(1, hi, u, s + 1)

    def rows_of(s):
        pair = pair_of(s)
        x0 = xbuf[2 * pair].astype(F32)
        x1 = xbuf[2 * pair + 1].astype(F32)
        rows = []
        for g in range(8):
            rows += [x0[g * 8 : g * 8 + 8], x1[g * 8 : g * 8 + 8]]
        return jnp.concatenate(rows, axis=0)

    def forward(s, part):
        slot = lax.rem(s, 4)
        if part == 0:

            @pl.when(s == 0)
            def _():
                for m, c in enumerate((gate_c, up_c)):
                    take(wbuf.at[theirs, c], w_recv.at[m])
                take(hgb, l_sem.at[2])

            xp = rows_of(s).astype(BF16)
            xcur[s] = xp
            blocks = range(CY // 256, wide // 256)
        else:
            xp = xcur[s]
            blocks = range(CY // 256)
        for n in blocks:
            c = slice(n * 256, (n + 1) * 256)
            part_sum = jnp.dot(xp, wbuf[:, c], preferred_element_type=F32).reshape(2, 4, 16, 256)
            fbuf[slot, :, :, :, c] = part_sum
            sbuf[s, :, :, :, c] = part_sum.astype(BF16)
        if part == 0:
            send(sbuf.at[s, xo, :, :, x_c], ux.at[s], ssem.at[3, s], rsem.at[3, s], over_x)
        else:
            for k in (1, 2, 3):
                send(
                    sbuf.at[s, :, row_of(k), :, y_c], gyb.at[s, k - 1],
                    ssem.at[k - 1, s], rsem.at[k - 1, s], at_y(k),
                )

    def reduce_b(s):
        slot = lax.rem(s, 4)
        take(ux.at[s], rsem.at[3, s])
        total = fbuf[slot, xl, :, :, CY:] + ux[s].astype(F32)
        uacc[slot] = total
        us[s] = total.astype(BF16)
        for k in (1, 2, 3):
            send(us.at[s, row_of(k)], uyb.at[s, k - 1], ssem.at[4 + k, s], rsem.at[4 + k, s], at_y(k))
        for k in (1, 2, 3):
            take(gyb.at[s, k - 1], rsem.at[k - 1, s])

        def side(xx):
            total = fbuf[slot, xx, y, :, :CY]
            for k in range(3):
                total += gyb[s, k, xx].astype(F32)
            return total

        gxs[s] = side(xo).astype(BF16)
        send(gxs.at[s], gxr.at[s], ssem.at[4, s], rsem.at[4, s], over_x)
        gown[slot] = side(xl)

    def reduce_c(s):
        slot = lax.rem(s, 4)
        rows = pl.ds(pl.multiple_of(pair_of(s) * 16, 16), 16)
        for k in (1, 2, 3):
            take(uyb.at[s, k - 1], rsem.at[4 + k, s])
        take(gxr.at[s], rsem.at[4, s])
        first = gown[slot] + gxr[s].astype(F32)
        second = uacc[slot, y]
        for k in range(3):
            second += uyb[s, k].astype(F32)
        full = jnp.concatenate([first, second], axis=1)
        gate, up = full[:, :cols], full[:, cols:]
        sig = jax.nn.sigmoid(gate)
        act = gate * sig
        hidb[rows, :] = (act * up).astype(BF16)
        cot = hgb[rows, :].astype(F32)
        dbuf[s, xl, y, :, :cols] = (cot * up * sig * (1.0 + gate * (1.0 - sig))).astype(BF16)
        dbuf[s, xl, y, :, cols:] = (cot * act).astype(BF16)

    def order(i):
        return jnp.where(i < FIRST, i, NS - 1 + FIRST - i)

    def same(ref, kind, s, device):
        send(ref, ref, ssem.at[kind, s], rsem.at[kind, s], device)

    def spread_a(s):
        same(dbuf.at[s, xl, y, :, y_c], 8, s, over_x)
        for k in (1, 2, 3):
            same(dbuf.at[s, xl, y, :, x_c], 8 + k, s, at_y(k))

    def spread_b(s):
        take(dbuf.at[s, xo, y, :, y_c], rsem.at[8, s])
        for k in (1, 2, 3):
            same(dbuf.at[s, :, y, :, y_c], 11 + k, s, at_y(k))
        for k in (1, 2, 3):
            take(dbuf.at[s, xl, row_of(4 - k), :, x_c], rsem.at[8 + k, s])
        same(dbuf.at[s, xl, :, :, x_c], 15, s, over_x)

    def spread_c(s, part):
        if part == 0:
            for k in (1, 2, 3):
                take(dbuf.at[s, :, row_of(4 - k), :, y_c], rsem.at[11 + k, s])
            take(dbuf.at[s, xo, :, :, x_c], rsem.at[15, s])
        pair = pair_of(s)
        delta = dbuf[s].reshape(128, wide)
        width = dc // 2
        for n in range(part * width // 256, (part + 1) * width // 256):
            c = slice(n * 256, (n + 1) * 256)
            piece = lax.dot_general(
                delta, wt[:, c], (((1,), (0,)), ((), ())), preferred_element_type=F32
            )
            for g in range(8):
                for q in range(2):
                    r = g * 16 + q * 8
                    pbuf[2 * pair + q, g * 8 : g * 8 + 8, c] = piece[r : r + 8]

    def ring(side, r, u):
        dest = lax.rem(z + NZ - 8 + r, NZ) if side == 0 else lax.rem(z + 7 - r, NZ)
        limit = (8 if side == 0 else 7) - LOW
        device = down_z if side == 0 else up_z
        rows = pl.ds(u * SUB, SUB)
        zacc[...] = pbuf[dest, rows, :]

        @pl.when(r > 0)
        def _():
            take(zr.at[side, r - 1, rows], z_recv.at[side, r - 1, u])
            zacc[...] += zr[side, r - 1, rows].astype(F32)

        @pl.when(r - 1 >= limit)
        def _():
            take(zrl.at[side, r - 1 - limit, rows], zl_recv.at[side, r - 1 - limit, u])
            zacc[...] += zrl[side, r - 1 - limit, rows].astype(F32)

        total = zacc[...]
        top = total.astype(BF16)
        zs[side, r, rows] = top
        send(zs.at[side, r, rows], zr.at[side, r, rows], z_send.at[side, r, u], z_recv.at[side, r, u], device)

        @pl.when(r >= limit)
        def _():
            zsl[side, r - limit, rows] = (total - top.astype(F32)).astype(BF16)
            send(
                zsl.at[side, r - limit, rows], zrl.at[side, r - limit, rows],
                zl_send.at[side, r - limit, u], zl_recv.at[side, r - limit, u], device,
            )

    def reduce_z(r, part):
        for u in part:
            ring(0, r, u)

            @pl.when(r > 0)
            def _():
                ring(1, r - 1, u)

    def end_z():
        for u in range(NU):
            rows = pl.ds(u * SUB, SUB)
            total = pbuf[z, rows, :]
            for side, last in ((0, 7), (1, 6)):
                take(zr.at[side, last, rows], z_recv.at[side, last, u])
                total += zr[side, last, rows].astype(F32)
                take(zrl.at[side, LOW - 1, rows], zl_recv.at[side, LOW - 1, u])
                total += zrl[side, LOW - 1, rows].astype(F32)
            for i in range(SUB // 8):
                g = u * (SUB // 8) + i
                fs[0, g] = total[i * 8 : i * 8 + 4]
                fs[1, g] = total[i * 8 + 4 : i * 8 + 8]
        for j, h in plane:
            g, hh, device = to_plane(j, h)
            send(fs.at[hh, g], fr.at[xh, p], f_send.at[h, j], f_recv.at[h, j], device)
        fr[xh, p] = fs[xh, p]

    def turn(s):
        xpt[:, pl.ds(pl.multiple_of(s * 128, 128), 128)] = xcur[s].T

    w_part = (pl.ds(0, 1024), pl.ds(1024, wide - 1024))

    def weight_half(w):
        owner = jnp.where(w == 0, 1 - core, core)
        x = xpt[pl.ds(pl.multiple_of(owner * half, half), half), :]
        for n in range(wide // 256):
            c = slice(n * 256, (n + 1) * 256)
            total = jnp.dot(x, dbuf[:, :, :, :, c].reshape(NS * 128, 256), preferred_element_type=F32)

            @pl.when(w == 0)
            def _():
                ws[:, c] = total.astype(BF16)

            @pl.when(w == 1)
            def _():
                wown[:, c] = total

            if n in (3, wide // 256 - 1):
                q = 0 if n == 3 else 1

                @pl.when(w == 0)
                def _():
                    send(ws.at[:, w_part[q]], wr.at[:, w_part[q]], ww_send.at[q], ww_recv.at[q], over_c)

    def turn_weights(i):
        for k in range(TURNS):
            n = i * TURNS + k

            @pl.when(n < wide // 128)
            def _():
                c = pl.ds(pl.multiple_of(n * 128, 128), 128)
                wt[c, :] = wbuf[:, c].T

    def when(lo, hi, t, body):
        @pl.when(jnp.logical_and(t >= lo, t < hi))
        def _():
            body(t - lo)

    start2 = 12 - FIRST

    def gather_at(t, u):
        when(0, 8, t, lambda s: gather_z(s, range(u, u + 1)))

    def ring_at(t, u):
        when(15, 23, t, lambda r: reduce_z(r, range(u, u + 1)))

    def step(t, carry):
        ring_at(t, 0)
        gather_at(t, 0)
        when(5, 13, t, reduce_c)
        when(start2, start2 + 8, t, lambda i: spread_a(order(i)))
        gather_at(t, 1)
        when(3, 11, t, reduce_b)
        when(start2 + 1, start2 + 9, t, lambda i: spread_b(order(i)))
        ring_at(t, 1)
        gather_at(t, 2)
        when(1, 9, t, lambda s: forward(s, 0))
        when(start2 + 2, start2 + 10, t, lambda i: spread_c(order(i), 0))
        ring_at(t, 2)
        gather_at(t, 3)
        when(1, 9, t, lambda s: forward(s, 1))
        when(start2 + 2, start2 + 10, t, lambda i: spread_c(order(i), 1))
        ring_at(t, 3)
        when(23, 24, t, lambda i: end_z())
        when(22, 24, t, weight_half)
        when(8, 16, t, turn)
        when(9, 14, t, turn_weights)
        return carry

    lax.fori_loop(0, 24, step, 0)

    pltpu.make_async_copy(hidb, hid_ref, o_sem.at[0]).start()
    for q in range(2):
        take(wr.at[:, w_part[q]], ww_recv.at[q])
        wout[:, w_part[q]] = (wown[:, w_part[q]] + wr[:, w_part[q]].astype(F32)).astype(BF16)
        if q == 0:
            pltpu.make_async_copy(wout.at[:, gate_c], gg_ref, o_sem.at[1]).start()
    pltpu.make_async_copy(wout.at[:, up_c], ug_ref, o_sem.at[2]).start()
    for j, h in plane:
        take(fr.at[lax.rem(xh + h, 2), lax.rem(p + 8 - j, 8)], f_recv.at[h, j])
    for g in range(8):
        tg_ref[:, g * dc : (g + 1) * dc] = (fr[0, g] + fr[1, g]).astype(BF16)

    for j, h in plane:
        take(ts.at[0], t_send.at[h, j])
        take(fs.at[0, 0], f_send.at[h, j])
    for m, c in enumerate((gate_c, up_c)):
        take(wbuf.at[mine, c], w_send.at[m])
    for q in range(2):
        take(ws.at[:, w_part[q]], ww_send.at[q])

    def drain(s, carry):
        for u in range(NU):
            take(block(0, u), az_send.at[0, s, u])
            take(zs.at[0, s, pl.ds(u * SUB, SUB)], z_send.at[0, s, u])

            @pl.when(s < 7)
            def _():
                take(block(0, u), az_send.at[1, s, u])
                take(zs.at[1, s, pl.ds(u * SUB, SUB)], z_send.at[1, s, u])

            @pl.when(s < LOW)
            def _():
                for side in range(2):
                    take(zsl.at[side, s, pl.ds(u * SUB, SUB)], zl_send.at[side, s, u])

        for k in range(3):
            take(gyb.at[s, k], ssem.at[k, s])
            take(uyb.at[s, k], ssem.at[5 + k, s])
            take(uyb.at[s, k], ssem.at[9 + k, s])
            take(gyb.at[s, k], ssem.at[12 + k, s])
        take(ux.at[s], ssem.at[3, s])
        take(gxs.at[s], ssem.at[4, s])
        take(gxs.at[s], ssem.at[8, s])
        take(ux.at[s], ssem.at[15, s])
        return carry

    lax.fori_loop(0, NS, drain, 0)
    take(hidb, o_sem.at[0])
    take(wout.at[:, gate_c], o_sem.at[1])
    take(wout.at[:, up_c], o_sem.at[2])


def finish(*refs):
    for src, dst in zip(refs[:4], refs[4:]):
        dst[...] = src[...]


def per_device(tokens, gate_weight, up_weight, hidden_grad):
    half, cols = gate_weight.shape
    rows = tokens.shape[0]
    dc = 2 * half
    wide = 2 * cols
    cx = wide - CY
    group = hidden_grad.shape[0]
    v = pltpu.VMEM
    dma = pltpu.SemaphoreType.DMA
    scratch = [
        v((dc, wide), BF16),
        v((wide, dc), BF16),
        v((8, rows, dc), BF16), v((2, 8, rows, dc), BF16),
        v((64, dc), F32),
        v((NZ, 64, dc), BF16),
        v((NS, 128, dc), BF16),
        v((dc, NS * 128), BF16),
        v((group, cols), BF16), v((group, cols), BF16),
        v((NS, 2, 4, 16, wide), BF16),
        v((4, 2, 4, 16, wide), F32),
        v((NS, 3, 2, 16, CY), BF16),
        v((NS, 16, CY), BF16), v((NS, 16, CY), BF16),
        v((4, 16, CY), F32),
        v((NS, 4, 16, cx), BF16),
        v((4, 4, 16, cx), F32),
        v((NS, 4, 16, cx), BF16),
        v((NS, 3, 16, cx), BF16),
        v((NS, 2, 4, 16, wide), BF16),
        v((NZ, 64, dc), F32),
        v((SUB, dc), F32),
        v((2, 8, 64, dc), BF16), v((2, 8, 64, dc), BF16),
        v((2, LOW, 64, dc), BF16), v((2, LOW, 64, dc), BF16),
        v((2, 8, rows, dc), F32), v((2, 8, rows, dc), F32),
        v((half, wide), BF16), v((half, wide), BF16),
        v((half, wide), F32),
        v((half, wide), BF16),
        dma((3,)), dma((2,)), dma((2,)),
        dma((2, 8)), dma((2, 8)),
        dma((2, 8, NU)), dma((2, 8, NU)),
        dma((16, NS)), dma((16, NS)),
        dma((2, 8, NU)), dma((2, 8, NU)),
        dma((2, LOW, NU)), dma((2, LOW, NU)),
        dma((2, 8)), dma((2, 8)),
        dma((2,)), dma((2,)),
        dma((3,)),
    ]
    vm = pl.BlockSpec(memory_space=pltpu.VMEM)
    hbm = pl.BlockSpec(memory_space=pl.ANY)
    shapes = (
        jax.ShapeDtypeStruct((group, cols), BF16),
        jax.ShapeDtypeStruct(tokens.shape, BF16),
        jax.ShapeDtypeStruct((half, cols), BF16),
        jax.ShapeDtypeStruct((half, cols), BF16),
    )
    results = pl.pallas_call(
        kernel,
        out_shape=shapes,
        in_specs=[vm, hbm, hbm, hbm],
        out_specs=(hbm, vm, hbm, hbm),
        scratch_shapes=scratch,
        compiler_params=pltpu.CompilerParams(
            collective_id=0, has_side_effects=True, vmem_limit_bytes=60 * 1024 * 1024
        ),
        cost_estimate=pl.CostEstimate(flops=11_300_000_000, bytes_accessed=6_000_000, transcendentals=114_688),
    )(tokens, gate_weight, up_weight, hidden_grad)
    return pl.pallas_call(
        finish,
        out_shape=shapes,
        in_specs=[vm] * 4,
        out_specs=(vm,) * 4,
    )(*results)


def solution(mesh):
    placed = (P(("dp", "tensor"), None), P("dp", "tensor"), P("dp", "tensor"), P("dp", "tensor"))
    return jax.shard_map(
        per_device,
        mesh=mesh,
        in_specs=placed,
        out_specs=(
            P("dp", "tensor"),
            P(("dp", "tensor"), None),
            P("dp", "tensor"),
            P("dp", "tensor"),
        ),
        check_vma=False,
    )
```
